512 devices in a mesh: grp: 8 (over x, z_hi), blk: 64 (over z_lo, y, core).
Axes of the slice: x: 4, y: 4, z: 16 (z_hi: 2, z_lo: 8; z = z_hi * 8 + z_lo), core: 2. Of those that a mesh axis runs over, the one named last changes fastest.
Arguments:
- grad: bfloat16 [320, 16384], P(None, ('grp', 'blk')), may hold values from -6 to 6
- moment: float32 [320, 16384], P(None, ('grp', 'blk')), may hold values from -4 to 4
- second_moment: float32 [320, 16384], P('grp', 'blk'), may hold values from 0.01 to 1
- left_basis: bfloat16 [320, 320], replicated, may hold values from -0.3125 to 0.3125
- right_basis: bfloat16 [16384, 16384], P('grp', 'blk'), may hold values from -0.046875 to 0.046875
Outputs:
- momentum: float32 [320, 16384], P(None, ('grp', 'blk'))
- second: float32 [320, 16384], P('grp', 'blk')
- update: float32 [320, 16384], P(None, ('grp', 'blk'))
The draws below stay inside these ranges and needn't reach their ends.
All inputs are finite; a program needn't handle non-finite values.
Results may differ from the reference program's by a relative error of at most 0.0049.
Values may be sent and summed in bfloat16 or wider, within the bound.
No kernel may reach another device: no remote copies, remote signals or barrier semaphores. Data moves between devices by JAX's collectives and lax.ppermute only.
A program may use at most 64 MiB of HBM per device.

```python
import math
import jax
import jax.numpy as jnp
from jax import lax

ROWS = 320
N = 16384


def block_levels(stream_key, dims, split, smallest, largest):
    factor_of = 1.0
    for position, blocks in split:
        heights = jax.random.uniform(jax.random.fold_in(jax.random.fold_in(stream_key, 6), position), (blocks,), jnp.float32, smallest / len(split), largest / len(split))
        factor_of = factor_of * jnp.repeat(jnp.exp(heights), dims[position] // blocks).reshape((-1,) + (1,) * (len(dims) - 1 - position))
    return factor_of


def scatter_about(stream_key, dims, width, limit, pieces=(), dtype=jnp.bfloat16):
    result = jax.random.normal(stream_key, dims, jnp.float32) * width
    if len(pieces) > 0:
        result = block_levels(stream_key, dims, pieces, -0.22, 0.18) * result
    return jnp.clip(result, min=-limit, max=limit).astype(dtype)


def setup_inputs(seed: int = 0) -> dict:
    keys = jax.random.split(jax.random.key(seed), 6)
    return {
        "grad": scatter_about(keys[0], (ROWS, N), 1.0, 6.0, ((1, 512),)),
        "moment": scatter_about(keys[1], (ROWS, N), 0.5, 4.0, ((1, 512),), jnp.float32),
        "second_moment": jnp.clip(jnp.exp(math.log(1.0) - 4.6051702 * jax.random.uniform(keys[2], (ROWS, N), jnp.float32) ** block_levels(keys[2], (ROWS, N), ((0, 8), (1, 64)), -0.2, 0.2)), 0.01, 1.0),
        "left_basis": scatter_about(keys[3], (ROWS, ROWS), ROWS ** -0.5, 0.3125),
        "right_basis": scatter_about(keys[4], (N, N), N ** -0.5, 0.046875, ((0, 8), (1, 64))),
    }


beta_first = 0.95
beta_second = 0.95
epsilon_root = 1e-08

def reference(grad, moment, second_moment, left_basis, right_basis):
    momentum = beta_first * moment + (1.0 - beta_first) * grad.astype(jnp.float32)
    momentum_bf = momentum.astype(jnp.bfloat16)
    left_grad = jnp.dot(left_basis.T, grad, preferred_element_type=jnp.float32).astype(jnp.bfloat16)
    left_moment = jnp.dot(left_basis.T, momentum_bf, preferred_element_type=jnp.float32).astype(jnp.bfloat16)
    rot_grad = jnp.dot(left_grad, right_basis, preferred_element_type=jnp.float32)
    rot_moment = jnp.dot(left_moment, right_basis, preferred_element_type=jnp.float32)
    second = beta_second * second_moment + (1.0 - beta_second) * rot_grad * rot_grad
    direction = (rot_moment / (jnp.sqrt(second) + epsilon_root)).astype(jnp.bfloat16)
    back = lax.dot_general(direction, right_basis, (((1,), (1,)), ((), ())), preferred_element_type=jnp.float32).astype(jnp.bfloat16)
    update = jnp.dot(left_basis, back, preferred_element_type=jnp.float32)
    return (momentum, second, update)
```

```python
import jax
import jax.numpy as jnp
from jax import lax
from jax.sharding import Mesh, PartitionSpec as P

beta_first = 0.95
beta_second = 0.95
epsilon_root = 1e-08

f32 = jnp.float32
bf16 = jnp.bfloat16
X, ZH, ZL, Y, C = 4, 2, 8, 4, 2
SWAP = [(0, 1), (1, 0)]


def left_rotate(values, left_basis):
    return lax.dot_general(
        values, left_basis, (((0,), (0,)), ((), ())), preferred_element_type=f32
    ).astype(bf16)


def spread(values, axis, count):
    return lax.all_to_all(
        jnp.broadcast_to(values[None], (count,) + values.shape), axis, 0, 0
    )


def add_up(values):
    return jnp.sum(values.astype(f32), axis=0)


def per_device(grad, moment, second_moment, left_basis, right_basis):
    core = lax.axis_index("core")
    momentum = beta_first * moment + (1.0 - beta_first) * grad.astype(f32)
    left = jnp.concatenate(
        [left_rotate(grad, left_basis), left_rotate(momentum.astype(bf16), left_basis)], axis=1
    )
    by_core = right_basis.reshape(ZL, Y, C, 32, 256)

    def rows_of(which):
        part = lax.dynamic_index_in_dim(by_core, which, 2, keepdims=False)
        return part.transpose(1, 0, 2, 3).reshape(1024, 256)

    right_own, right_other = rows_of(core), rows_of(1 - core)

    left = spread(left, "zl", ZL)
    left = spread(left.reshape(256, 640), "y", Y).reshape(1024, 640)
    left_other = lax.ppermute(left, "core", SWAP)

    def rotate(piece, basis):
        return lax.dot_general(piece, basis, (((0,), (0,)), ((), ())), preferred_element_type=f32)

    part = rotate(left, right_own) + rotate(left_other, right_other)
    part = part.reshape(2, 8, 40, 256).transpose(1, 0, 2, 3).astype(bf16)
    summed = add_up(lax.all_to_all(part, ("x", "zh"), 0, 0))
    second = beta_second * second_moment + (1.0 - beta_second) * summed[0] * summed[0]
    direction = (summed[1] / (jnp.sqrt(second) + epsilon_root)).astype(bf16)
    direction = spread(direction, ("x", "zh"), X * ZH).reshape(320, 256)

    def back_rotate(basis):
        return lax.dot_general(
            basis, direction, (((1,), (1,)), ((), ())), preferred_element_type=f32
        )

    sent = lax.ppermute(back_rotate(right_other).astype(bf16), "core", SWAP)
    back = back_rotate(right_own) + sent.astype(f32)
    back = lax.all_to_all(back.astype(bf16).reshape(Y, ZL * 32, 320), "y", 0, 0)
    back = add_up(back).astype(bf16).reshape(ZL, 32, 320)
    back = add_up(lax.all_to_all(back, "zl", 0, 0)).astype(bf16)
    update = lax.dot_general(
        left_basis, back, (((1,), (1,)), ((), ())), preferred_element_type=f32
    )
    return (momentum, second, update)


def solution(mesh):
    names = ("x", "zh", "zl", "y", "core")
    fine = Mesh(mesh.devices.reshape(X, ZH, ZL, Y, C), names)
    columns = P(None, names)
    block = P(("x", "zh"), ("zl", "y", "core"))
    return jax.shard_map(
        per_device,
        mesh=fine,
        in_specs=(columns, columns, block, P(), block),
        out_specs=(columns, block, columns),
        check_vma=False,
    )
```

```python
import jax
import jax.numpy as jnp
from jax import lax
from jax.sharding import Mesh, PartitionSpec as P

beta_first = 0.95
beta_second = 0.95
epsilon_root = 1e-08

f32 = jnp.float32
bf16 = jnp.bfloat16
X, ZH, ZA, ZB, Y, C = 4, 2, 4, 2, 4, 2
SWAP = [(0, 1), (1, 0)]


def left_rotate(values, left_basis):
    return lax.dot_general(
        values, left_basis, (((0,), (0,)), ((), ())), preferred_element_type=f32
    ).astype(bf16)


def spread(values, axis, count):
    return lax.all_to_all(
        jnp.broadcast_to(values[None], (count,) + values.shape), axis, 0, 0
    )


def add_up(values):
    return jnp.sum(values.astype(f32), axis=0)


def per_device(grad, moment, second_moment, left_basis, right_basis):
    core = lax.axis_index("core")
    half = lax.axis_index("zh")
    momentum = beta_first * moment + (1.0 - beta_first) * grad.astype(f32)
    left = jnp.concatenate(
        [left_rotate(grad, left_basis), left_rotate(momentum.astype(bf16), left_basis)], axis=1
    )
    by_core = right_basis.reshape(ZA, ZB * Y, C, 32, 256)

    def rows_of(which):
        part = lax.dynamic_index_in_dim(by_core, which, 2, keepdims=False)
        return part.transpose(1, 0, 2, 3).reshape(1024, 256)

    right_own, right_other = rows_of(core), rows_of(1 - core)

    left = spread(left, "za", ZA)
    left = spread(left.reshape(128, 640), ("zb", "y"), ZB * Y).reshape(1024, 640)
    left_other = lax.ppermute(left, "core", SWAP)

    def rotate(piece, basis):
        return lax.dot_general(piece, basis, (((0,), (0,)), ((), ())), preferred_element_type=f32)

    part = rotate(left, right_own) + rotate(left_other, right_other)
    part = part.reshape(2, X, 80, 256).transpose(1, 0, 2, 3).astype(bf16)
    part = add_up(lax.all_to_all(part, "x", 0, 0))
    other = lax.ppermute(
        jnp.concatenate([part.reshape(160, 256), second_moment]).astype(bf16), "zh", SWAP
    ).astype(f32)
    summed = (part + other[:160].reshape(2, 80, 256)).reshape(2, ZH, 40, 256)
    mine = jnp.arange(ZH)[:, None, None] == half
    second_moments = jnp.where(mine, second_moment[None], other[None, 160:])
    second = beta_second * second_moments + (1.0 - beta_second) * summed[0] * summed[0]
    direction = (summed[1] / (jnp.sqrt(second) + epsilon_root)).astype(bf16)
    second = lax.dynamic_index_in_dim(second, half, 0, keepdims=False)
    direction = spread(direction.reshape(80, 256), "x", X).reshape(320, 256)

    def back_rotate(basis):
        return lax.dot_general(
            basis, direction, (((1,), (1,)), ((), ())), preferred_element_type=f32
        )

    sent = lax.ppermute(back_rotate(right_other).astype(bf16), "core", SWAP)
    back = back_rotate(right_own) + sent.astype(f32)
    back = lax.all_to_all(back.astype(bf16).reshape(ZB * Y, ZA * 32, 320), ("zb", "y"), 0, 0)
    back = add_up(back).astype(bf16).reshape(ZA, 32, 320)
    back = add_up(lax.all_to_all(back, "za", 0, 0)).astype(bf16)
    update = lax.dot_general(
        left_basis, back, (((1,), (1,)), ((), ())), preferred_element_type=f32
    )
    return (momentum, second, update)


def solution(mesh):
    names = ("x", "zh", "za", "zb", "y", "core")
    fine = Mesh(mesh.devices.reshape(X, ZH, ZA, ZB, Y, C), names)
    columns = P(None, names)
    block = P(("x", "zh"), ("za", "zb", "y", "core"))
    return jax.shard_map(
        per_device,
        mesh=fine,
        in_specs=(columns, columns, block, P(), block),
        out_specs=(columns, block, columns),
        check_vma=False,
    )
```

```python
import jax
import jax.numpy as jnp
from jax import lax
from jax.experimental import pallas as pl
from jax.experimental.pallas import tpu as pltpu
from jax.sharding import Mesh, PartitionSpec as P

beta_first = 0.95
beta_second = 0.95
epsilon_root = 1e-08

f32 = jnp.float32
bf16 = jnp.bfloat16
X, ZH, ZA, ZB, Y, C = 4, 2, 4, 2, 4, 2
SWAP = [(0, 1), (1, 0)]
VMEM = pl.BlockSpec(memory_space=pltpu.VMEM)
SMEM = pl.BlockSpec(memory_space=pltpu.SMEM)


def dot(left, right, over_left, over_right):
    return lax.dot_general(
        left, right, (((over_left,), (over_right,)), ((), ())), preferred_element_type=f32
    )


def local(body, outs, ins, scalars=0):
    shapes = tuple(jax.ShapeDtypeStruct(shape, dtype) for shape, dtype in outs)
    return pl.pallas_call(
        body,
        out_shape=shapes,
        in_specs=[SMEM] * scalars + [VMEM] * (len(ins) - scalars),
        out_specs=(VMEM,) * len(outs),
        compiler_params=pltpu.CompilerParams(vmem_limit_bytes=24 << 20),
    )(*ins)


def left_kernel(grad, moment, basis, momentum, sent):
    new = beta_first * moment[...] + (1.0 - beta_first) * grad[...].astype(f32)
    momentum[...] = new
    rotated_grad = dot(grad[...], basis[...], 1, 0).astype(bf16)
    rotated_moment = dot(new.astype(bf16), basis[...], 1, 0).astype(bf16)
    for i in range(ZA):
        sent[i, :, :320] = rotated_grad
        sent[i, :, 320:] = rotated_moment


def rows_of(basis, core):
    return jnp.concatenate(
        [basis[za * ZB * Y + k, core] for k in range(ZB * Y) for za in range(ZA)], axis=0
    )


def rotate_own_kernel(core, left, basis, part):
    part[...] = dot(left[...], rows_of(basis, core[0]), 0, 0)


def rotate_other_kernel(core, left, basis, part, sent):
    total = (part[...] + dot(left[...], rows_of(basis, 1 - core[0]), 0, 0)).astype(bf16)
    for x in range(X):
        sent[x, :80] = total[x * 80 : x * 80 + 80]
        sent[x, 80:] = total[320 + x * 80 : 400 + x * 80]


def sum_kernel(parts, second_moment, total, sent):
    value = jnp.sum(parts[...].astype(f32), axis=0)
    total[...] = value
    sent[...] = jnp.concatenate([value, second_moment[...]], axis=0).astype(bf16)


def direction_kernel(half, total, other, second_moment, second, sent):
    upper = half[0] == 0
    partner = other[...].astype(f32)
    summed = total[...] + partner[:160]
    mine, theirs = second_moment[...], partner[160:]
    before = jnp.where(
        upper, jnp.concatenate([mine, theirs], axis=0), jnp.concatenate([theirs, mine], axis=0)
    )
    after = beta_second * before + (1.0 - beta_second) * summed[:80] * summed[:80]
    second[...] = jnp.where(upper, after[:40], after[40:])
    direction = (summed[80:] / (jnp.sqrt(after) + epsilon_root)).astype(bf16)
    for i in range(X):
        sent[i] = direction


def back_other_kernel(core, direction, basis, sent):
    back = dot(direction[...], rows_of(basis, 1 - core[0]), 1, 1).astype(bf16)
    for k in range(ZB * Y):
        sent[k] = back[:, k * 128 : k * 128 + 128]


def back_own_kernel(core, direction, basis, received, sent):
    back = dot(direction[...], rows_of(basis, core[0]), 1, 1)
    for k in range(ZB * Y):
        sent[k] = (back[:, k * 128 : k * 128 + 128] + received[k].astype(f32)).astype(bf16)


def update_kernel(parts, basis, sent):
    back = jnp.sum(parts[...].astype(f32), axis=0).T.astype(bf16)
    update = dot(back, basis[...], 1, 1).astype(bf16)
    for i in range(ZA):
        sent[i] = update[i * 32 : i * 32 + 32]


def add_kernel(parts, total):
    total[...] = jnp.sum(parts[...].astype(f32), axis=0)


def spread(values, axis, count):
    return lax.all_to_all(
        jnp.broadcast_to(values[None], (count,) + values.shape), axis, 0, 0
    )


def per_device(grad, moment, second_moment, left_basis, right_basis):
    core = lax.axis_index("core").reshape(1)
    half = lax.axis_index("zh").reshape(1)
    basis = right_basis.reshape(ZA * ZB * Y, C, 32, 256)
    momentum, left = local(
        left_kernel,
        (((32, 320), f32), ((ZA, 32, 640), bf16)),
        (grad.T, moment.T, left_basis),
    )
    left = lax.all_to_all(left, "za", 0, 0).reshape(128, 640)
    left = spread(left, ("zb", "y"), ZB * Y).reshape(1024, 640)
    left_other = lax.ppermute(left, "core", SWAP)
    (part,) = local(rotate_own_kernel, (((640, 256), f32),), (core, left, basis), 1)
    (part,) = local(
        rotate_other_kernel, (((X, 160, 256), bf16),), (core, left_other, basis, part), 1
    )
    part = lax.all_to_all(part, "x", 0, 0)
    part, sent = local(
        sum_kernel, (((160, 256), f32), ((200, 256), bf16)), (part, second_moment)
    )
    other = lax.ppermute(sent, "zh", SWAP)
    second, direction = local(
        direction_kernel,
        (((40, 256), f32), ((X, 80, 256), bf16)),
        (half, part, other, second_moment),
        1,
    )
    direction = lax.all_to_all(direction, "x", 0, 0).reshape(320, 256)
    blocks = (((ZB * Y, 320, 128), bf16),)
    (sent,) = local(back_other_kernel, blocks, (core, direction, basis), 1)
    received = lax.ppermute(sent, "core", SWAP)
    (back,) = local(back_own_kernel, blocks, (core, direction, basis, received), 1)
    back = lax.all_to_all(back, ("zb", "y"), 0, 0)
    (update,) = local(update_kernel, (((ZA, 32, 320), bf16),), (back, left_basis))
    update = lax.all_to_all(update, "za", 0, 0)
    (update,) = local(add_kernel, (((32, 320), f32),), (update,))
    return (momentum.T, second, update.T)


def solution(mesh):
    names = ("x", "zh", "za", "zb", "y", "core")
    fine = Mesh(mesh.devices.reshape(X, ZH, ZA, ZB, Y, C), names)
    columns = P(None, names)
    block = P(("x", "zh"), ("za", "zb", "y", "core"))
    return jax.shard_map(
        per_device,
        mesh=fine,
        in_specs=(columns, columns, block, P(), block),
        out_specs=(columns, block, columns),
        check_vma=False,
    )
```

```python
import jax
import jax.numpy as jnp
from jax import lax
from jax.experimental import pallas as pl
from jax.experimental.pallas import tpu as pltpu
from jax.sharding import Mesh, PartitionSpec as P

beta_first = 0.95
beta_second = 0.95
epsilon_root = 1e-08

f32 = jnp.float32
bf16 = jnp.bfloat16
X, ZH, ZA, ZB, Y, C = 4, 2, 4, 2, 4, 2
SWAP = [(0, 1), (1, 0)]
VMEM = pl.BlockSpec(memory_space=pltpu.VMEM)
HBM = pl.BlockSpec(memory_space=pltpu.HBM)
SMEM = pl.BlockSpec(memory_space=pltpu.SMEM)


def dot(left, right, over_left, over_right):
    return lax.dot_general(
        left, right, (((over_left,), (over_right,)), ((), ())), preferred_element_type=f32
    )


def local(body, outs, ins, scalars=0):
    shapes = tuple(jax.ShapeDtypeStruct(shape, dtype) for shape, dtype in outs)
    return pl.pallas_call(
        body,
        out_shape=shapes,
        in_specs=[SMEM] * scalars + [VMEM] * (len(ins) - scalars),
        out_specs=(VMEM,) * len(outs),
        compiler_params=pltpu.CompilerParams(vmem_limit_bytes=24 << 20),
    )(*ins)


def left_kernel(grad_hbm, moment_hbm, basis_hbm, momentum, sent, grad, moment, basis, sems):
    pairs = ((grad_hbm, grad), (basis_hbm, basis), (moment_hbm, moment))
    copies = [
        pltpu.make_async_copy(source, target, sems.at[i])
        for i, (source, target) in enumerate(pairs)
    ]
    for copy in copies:
        copy.start()
    for copy in copies:
        copy.wait()
    new = beta_first * moment[...] + (1.0 - beta_first) * grad[...].astype(f32)
    momentum[...] = new
    rotated_grad = dot(grad[...], basis[...], 1, 0).astype(bf16)
    rotated_moment = dot(new.astype(bf16), basis[...], 1, 0).astype(bf16)
    for i in range(ZA):
        sent[i, :, :320] = rotated_grad
        sent[i, :, 320:] = rotated_moment


def left_stage(grad, moment, basis):
    return pl.pallas_call(
        left_kernel,
        out_shape=(
            jax.ShapeDtypeStruct((32, 320), f32),
            jax.ShapeDtypeStruct((ZA, 32, 640), bf16),
        ),
        in_specs=[HBM] * 3,
        out_specs=(VMEM, VMEM),
        scratch_shapes=[
            pltpu.VMEM((32, 320), bf16),
            pltpu.VMEM((32, 320), f32),
            pltpu.VMEM((320, 320), bf16),
            pltpu.SemaphoreType.DMA((3,)),
        ],
        compiler_params=pltpu.CompilerParams(vmem_limit_bytes=56 << 20),
    )(grad, moment, basis)


def kept_rows(basis, pair, core):
    return jnp.concatenate(
        [basis[za, pair, y, core] for y in range(Y) for za in range(ZA)], axis=0
    )


def received_rows(received, core):
    return jnp.concatenate(
        [received[za, y, core] for y in range(Y) for za in range(ZA)], axis=0
    )


def rotate_own_kernel(place, left, basis, received, part):
    core, pair = place[0], place[1]
    part[0] = dot(left[...], kept_rows(basis, pair, core), 0, 0)
    part[1] = dot(left[...], received_rows(received, core), 0, 0)


def rotate_other_kernel(place, left, basis, received, part, sent):
    core, pair = place[0], place[1]
    kept = part[0] + dot(left[...], kept_rows(basis, pair, 1 - core), 0, 0)
    given = part[1] + dot(left[...], received_rows(received, 1 - core), 0, 0)
    for to, total in ((pair, kept.astype(bf16)), (1 - pair, given.astype(bf16))):
        for x in range(X):
            sent[x * ZB + to, :80] = total[x * 80 : x * 80 + 80]
            sent[x * ZB + to, 80:] = total[320 + x * 80 : 400 + x * 80]


def sum_kernel(parts, second_moment, total, sent):
    value = jnp.sum(parts[...].astype(f32), axis=0)
    total[...] = value
    sent[...] = jnp.concatenate([value, second_moment[...]], axis=0).astype(bf16)


def direction_kernel(half, total, both, second_moment, second, sent):
    upper = half[0] == 0
    partner = both[1 - half[0]].astype(f32)
    summed = total[...] + partner[:160]
    mine, theirs = second_moment[...], partner[160:]
    before = jnp.where(
        upper, jnp.concatenate([mine, theirs], axis=0), jnp.concatenate([theirs, mine], axis=0)
    )
    after = beta_second * before + (1.0 - beta_second) * summed[:80] * summed[:80]
    second[...] = jnp.where(upper, after[:40], after[40:])
    direction = (summed[80:] / (jnp.sqrt(after) + epsilon_root)).astype(bf16)
    for i in range(X * ZB):
        sent[i] = direction


def back_rotate(pair, core, direction, basis, received):
    def columns(which):
        return jnp.concatenate([direction[x * ZB + which] for x in range(X)], axis=0)

    back = dot(columns(pair), kept_rows(basis, pair, core), 1, 1)
    return back + dot(columns(1 - pair), received_rows(received, core), 1, 1)


def back_other_kernel(place, direction, basis, received, sent):
    back = back_rotate(place[1], 1 - place[0], direction, basis, received).astype(bf16)
    for y in range(Y):
        sent[y] = back[:, y * 128 : y * 128 + 128]


def back_own_kernel(place, direction, basis, received, other, sent):
    back = back_rotate(place[1], place[0], direction, basis, received)
    for y in range(Y):
        sent[y] = (back[:, y * 128 : y * 128 + 128] + other[y].astype(f32)).astype(bf16)


def update_kernel(parts, basis, sent):
    back = jnp.sum(parts[...].astype(f32), axis=0).T.astype(bf16)
    update = dot(back, basis[...], 1, 1).astype(bf16)
    for i in range(ZA):
        sent[i] = update[i * 32 : i * 32 + 32]


def add_kernel(parts, total):
    total[...] = jnp.sum(parts[...].astype(f32), axis=0)


def spread(values, axis, count):
    return lax.all_to_all(
        jnp.broadcast_to(values[None], (count,) + values.shape), axis, 0, 0
    )


def per_device(grad, moment, second_moment, left_basis, right_basis):
    pair = lax.axis_index("zb")
    place = jnp.stack([lax.axis_index("core"), pair])
    half = lax.axis_index("zh").reshape(1)
    momentum, left = left_stage(grad.T, moment.T, left_basis)
    left = lax.all_to_all(left, "za", 0, 0).reshape(128, 640)
    basis = right_basis.reshape(ZA, ZB, Y, C, 32, 256)
    leaving = lax.dynamic_index_in_dim(basis, 1 - pair, 1, keepdims=False)
    received = lax.ppermute(leaving, "zb", SWAP)
    left = spread(left, "y", Y).reshape(512, 640)
    left, received = lax.optimization_barrier((left, received))
    left_other = lax.ppermute(left, "core", SWAP)
    (part,) = local(
        rotate_own_kernel, (((ZB, 640, 256), f32),), (place, left, basis, received), 1
    )
    (part,) = local(
        rotate_other_kernel,
        (((X * ZB, 160, 256), bf16),),
        (place, left_other, basis, received, part),
        1,
    )
    part = lax.all_to_all(part, ("x", "zb"), 0, 0)
    part, sent = local(
        sum_kernel, (((160, 256), f32), ((200, 256), bf16)), (part, second_moment)
    )
    both = lax.all_gather(sent, "zh")
    second, direction = local(
        direction_kernel,
        (((40, 256), f32), ((X * ZB, 80, 256), bf16)),
        (half, part, both, second_moment),
        1,
    )
    direction = lax.all_to_all(direction, ("x", "zb"), 0, 0)
    blocks = (((Y, 320, 128), bf16),)
    operands = (place, direction, basis, received)
    (sent,) = local(back_other_kernel, blocks, operands, 1)
    other = lax.ppermute(sent, "core", SWAP)
    (back,) = local(back_own_kernel, blocks, (*operands, other), 1)
    back = lax.all_to_all(back, "y", 0, 0)
    (update,) = local(update_kernel, (((ZA, 32, 320), bf16),), (back, left_basis))
    update = lax.all_to_all(update, "za", 0, 0)
    (update,) = local(add_kernel, (((32, 320), f32),), (update,))
    return (momentum.T, second, update.T)


def solution(mesh):
    names = ("x", "zh", "za", "zb", "y", "core")
    fine = Mesh(mesh.devices.reshape(X, ZH, ZA, ZB, Y, C), names)
    columns = P(None, names)
    block = P(("x", "zh"), ("za", "zb", "y", "core"))
    return jax.shard_map(
        per_device,
        mesh=fine,
        in_specs=(columns, columns, block, P(), block),
        out_specs=(columns, block, columns),
        check_vma=False,
    )
```

```python
import jax
import jax.numpy as jnp
from jax import lax
from jax.experimental import pallas as pl
from jax.experimental.pallas import tpu as pltpu
from jax.sharding import Mesh, PartitionSpec as P

beta_first = 0.95
beta_second = 0.95
epsilon_root = 1e-08

f32 = jnp.float32
bf16 = jnp.bfloat16
X, ZH, ZA, ZB, Y, C = 4, 2, 4, 2, 4, 2
SWAP = [(0, 1), (1, 0)]
VMEM = pl.BlockSpec(memory_space=pltpu.VMEM)
HBM = pl.BlockSpec(memory_space=pltpu.HBM)
SMEM = pl.BlockSpec(memory_space=pltpu.SMEM)


def dot(left, right, over_left, over_right):
    return lax.dot_general(
        left, right, (((over_left,), (over_right,)), ((), ())), preferred_element_type=f32
    )


def local(body, outs, ins, scalars=0):
    shapes = tuple(jax.ShapeDtypeStruct(shape, dtype) for shape, dtype in outs)
    return pl.pallas_call(
        body,
        out_shape=shapes,
        in_specs=[SMEM] * scalars + [VMEM] * (len(ins) - scalars),
        out_specs=(VMEM,) * len(outs),
        compiler_params=pltpu.CompilerParams(vmem_limit_bytes=24 << 20),
    )(*ins)


def left_kernel(grad_hbm, moment_hbm, basis_hbm, momentum, sent, grad, moment, basis, sems):
    pairs = ((grad_hbm, grad), (basis_hbm, basis), (moment_hbm, moment))
    copies = [
        pltpu.make_async_copy(source, target, sems.at[i])
        for i, (source, target) in enumerate(pairs)
    ]
    for copy in copies:
        copy.start()
    for copy in copies:
        copy.wait()
    new = beta_first * moment[...] + (1.0 - beta_first) * grad[...].astype(f32)
    momentum[...] = new
    rotated_grad = dot(grad[...], basis[...], 1, 0).astype(bf16)
    rotated_moment = dot(new.astype(bf16), basis[...], 1, 0).astype(bf16)
    for i in range(ZA):
        sent[i, :, :320] = rotated_grad
        sent[i, :, 320:] = rotated_moment


def left_stage(grad, moment, basis):
    return pl.pallas_call(
        left_kernel,
        out_shape=(
            jax.ShapeDtypeStruct((32, 320), f32),
            jax.ShapeDtypeStruct((ZA, 32, 640), bf16),
        ),
        in_specs=[HBM] * 3,
        out_specs=(VMEM, VMEM),
        scratch_shapes=[
            pltpu.VMEM((32, 320), bf16),
            pltpu.VMEM((32, 320), f32),
            pltpu.VMEM((320, 320), bf16),
            pltpu.SemaphoreType.DMA((3,)),
        ],
        compiler_params=pltpu.CompilerParams(vmem_limit_bytes=56 << 20),
    )(grad, moment, basis)


def kept_rows(basis, pair, core):
    return jnp.concatenate(
        [basis[za, pair, y, core] for y in range(Y) for za in range(ZA)], axis=0
    )


def received_rows(received, core):
    return jnp.concatenate(
        [received[za, y, core] for y in range(Y) for za in range(ZA)], axis=0
    )


def rotate_own_kernel(place, left, basis, received, part):
    core, pair = place[0], place[1]
    part[0] = dot(left[...], kept_rows(basis, pair, core), 0, 0)
    part[1] = dot(left[...], received_rows(received, core), 0, 0)


def rotate_other_kernel(place, left, basis, received, part, sent):
    core, pair = place[0], place[1]
    kept = part[0] + dot(left[...], kept_rows(basis, pair, 1 - core), 0, 0)
    given = part[1] + dot(left[...], received_rows(received, 1 - core), 0, 0)
    for to, total in ((pair, kept.astype(bf16)), (1 - pair, given.astype(bf16))):
        for x in range(X):
            sent[x * ZB + to, :80] = total[x * 80 : x * 80 + 80]
            sent[x * ZB + to, 80:] = total[320 + x * 80 : 400 + x * 80]


def sum_kernel(parts, second_moment, total, sent):
    value = jnp.sum(parts[...].astype(f32), axis=0)
    total[...] = value
    sent[...] = jnp.concatenate([value, second_moment[...]], axis=0).astype(bf16)


def direction_kernel(place, total, both, second_moment, second, sent):
    upper = place[2] == 0
    partner = both[1 - place[2]].astype(f32)
    summed = total[...] + partner[:160]
    mine, theirs = second_moment[...], partner[160:]
    before = jnp.where(
        upper, jnp.concatenate([mine, theirs], axis=0), jnp.concatenate([theirs, mine], axis=0)
    )
    after = beta_second * before + (1.0 - beta_second) * summed[:80] * summed[:80]
    second[...] = jnp.where(upper, after[:40], after[40:])
    direction = (summed[80:] / (jnp.sqrt(after) + epsilon_root)).astype(bf16)
    for i in range(X * ZB):
        sent[i] = direction


def back_rotate(pair, core, direction, basis, received):
    def columns(which):
        return jnp.concatenate([direction[x * ZB + which] for x in range(X)], axis=0)

    back = dot(columns(pair), kept_rows(basis, pair, core), 1, 1)
    return back + dot(columns(1 - pair), received_rows(received, core), 1, 1)


def back_other_kernel(place, direction, basis, received, sent):
    back = back_rotate(place[1], 1 - place[0], direction, basis, received).astype(bf16)
    for y in range(Y):
        sent[y] = back[:, y * 128 : y * 128 + 128]


def back_own_kernel(place, direction, basis, received, part):
    back = back_rotate(place[1], place[0], direction, basis, received)
    for y in range(Y):
        part[y] = back[:, y * 128 : y * 128 + 128]


def back_add_kernel(part, other, sent):
    sent[...] = (part[...] + other[...].astype(f32)).astype(bf16)


def update_kernel(parts, basis, sent):
    back = jnp.sum(parts[...].astype(f32), axis=0).T.astype(bf16)
    update = dot(back, basis[...], 1, 1).astype(bf16)
    for i in range(ZA):
        block = update[i * 32 : i * 32 + 32]
        to = ZA - 1 - i
        sent[to, :32] = block[:, :128]
        sent[to, 32:64] = block[:, 128:256]
        sent[to, 64:] = jnp.concatenate([block[:16, 256:], block[16:, 256:]], axis=1)


def add_kernel(parts, total):
    value = jnp.sum(parts[...].astype(f32), axis=0)
    total[:, :128] = value[:32]
    total[:, 128:256] = value[32:64]
    total[:16, 256:] = value[64:, :64]
    total[16:, 256:] = value[64:, 64:]


def spread(values, axis, count):
    return lax.all_to_all(
        jnp.broadcast_to(values[None], (count,) + values.shape), axis, 0, 0
    )


def per_device(grad, moment, second_moment, left_basis, right_basis):
    pair = lax.axis_index("zb")
    place = jnp.stack([lax.axis_index("core"), pair, lax.axis_index("zh")])
    momentum, left = left_stage(grad.T, moment.T, left_basis)
    left = lax.all_to_all(left, "za", 0, 0).reshape(128, 640)
    basis = right_basis.reshape(ZA, ZB, Y, C, 32, 256)
    leaving = lax.dynamic_index_in_dim(basis, 1 - pair, 1, keepdims=False)
    received = lax.ppermute(leaving, "zb", SWAP)
    left = spread(left, "y", Y).reshape(512, 640)
    left, received = lax.optimization_barrier((left, received))
    left_other = lax.ppermute(left, "core", SWAP)
    (part,) = local(
        rotate_own_kernel, (((ZB, 640, 256), f32),), (place, left, basis, received), 1
    )
    (part,) = local(
        rotate_other_kernel,
        (((X * ZB, 160, 256), bf16),),
        (place, left_other, basis, received, part),
        1,
    )
    part = lax.all_to_all(part, ("x", "zb"), 0, 0)
    part, sent = local(
        sum_kernel, (((160, 256), f32), ((200, 256), bf16)), (part, second_moment)
    )
    both = lax.all_gather(sent, "zh")
    second, direction = local(
        direction_kernel,
        (((40, 256), f32), ((X * ZB, 80, 256), bf16)),
        (place, part, both, second_moment),
        1,
    )
    direction = lax.all_to_all(direction, ("x", "zb"), 0, 0)
    blocks = (((Y, 320, 128), bf16),)
    operands = (place, direction, basis, received)
    (sent,) = local(back_other_kernel, blocks, operands, 1)
    other = lax.ppermute(sent, "core", SWAP)
    (part,) = local(back_own_kernel, (((Y, 320, 128), f32),), operands, 1)
    (back,) = local(back_add_kernel, blocks, (part, other))
    back = lax.all_to_all(back, "y", 0, 0)
    (update,) = local(update_kernel, (((ZA, 80, 128), bf16),), (back, left_basis))
    update = lax.all_to_all(update, "za", 0, 0, axis_index_groups=[[3, 2, 1, 0]])
    (update,) = local(add_kernel, (((32, 320), f32),), (update,))
    return (momentum.T, second, update.T)


def solution(mesh):
    names = ("x", "zh", "za", "zb", "y", "core")
    fine = Mesh(mesh.devices.reshape(X, ZH, ZA, ZB, Y, C), names)
    columns = P(None, names)
    block = P(("x", "zh"), ("za", "zb", "y", "core"))
    return jax.shard_map(
        per_device,
        mesh=fine,
        in_specs=(columns, columns, block, P(), block),
        out_specs=(columns, block, columns),
        check_vma=False,
    )
```

```python
import jax
import jax.numpy as jnp
from jax import lax
from jax.experimental import pallas as pl
from jax.experimental.pallas import tpu as pltpu
from jax.sharding import Mesh, PartitionSpec as P

beta_first = 0.95
beta_second = 0.95
epsilon_root = 1e-08

f32 = jnp.float32
bf16 = jnp.bfloat16
X, ZH, ZA, ZB, Y, C = 4, 2, 4, 2, 4, 2
SWAP = [(0, 1), (1, 0)]
ZA_ORDER = (3, 2, 1, 0)
Y_ORDER = (3, 2, 1, 0)
XZ_ORDER = (7, 6, 5, 4, 3, 2, 1, 0)
VMEM = pl.BlockSpec(memory_space=pltpu.VMEM)
HBM = pl.BlockSpec(memory_space=pltpu.HBM)
SMEM = pl.BlockSpec(memory_space=pltpu.SMEM)


def slot(x, pair):
    return X * ZB - 1 - x * ZB - pair


def dot(left, right, over_left, over_right):
    return lax.dot_general(
        left, right, (((over_left,), (over_right,)), ((), ())), preferred_element_type=f32
    )


def local(body, outs, ins, scalars=0):
    shapes = tuple(jax.ShapeDtypeStruct(shape, dtype) for shape, dtype in outs)
    return pl.pallas_call(
        body,
        out_shape=shapes,
        in_specs=[SMEM] * scalars + [VMEM] * (len(ins) - scalars),
        out_specs=(VMEM,) * len(outs),
        compiler_params=pltpu.CompilerParams(vmem_limit_bytes=24 << 20),
    )(*ins)


def left_kernel(grad_hbm, moment_hbm, basis_hbm, momentum, sent, grad, moment, basis, sems):
    pairs = ((grad_hbm, grad), (basis_hbm, basis), (moment_hbm, moment))
    copies = [
        pltpu.make_async_copy(source, target, sems.at[i])
        for i, (source, target) in enumerate(pairs)
    ]
    for copy in copies:
        copy.start()
    for copy in copies:
        copy.wait()
    new = beta_first * moment[...] + (1.0 - beta_first) * grad[...].astype(f32)
    momentum[...] = new
    rotated_grad = dot(grad[...], basis[...], 1, 0).astype(bf16)
    rotated_moment = dot(new.astype(bf16), basis[...], 1, 0).astype(bf16)
    for i in range(ZA):
        sent[i, :, :320] = rotated_grad
        sent[i, :, 320:] = rotated_moment


def left_stage(grad, moment, basis):
    return pl.pallas_call(
        left_kernel,
        out_shape=(
            jax.ShapeDtypeStruct((32, 320), f32),
            jax.ShapeDtypeStruct((ZA, 32, 640), bf16),
        ),
        in_specs=[HBM] * 3,
        out_specs=(VMEM, VMEM),
        scratch_shapes=[
            pltpu.VMEM((32, 320), bf16),
            pltpu.VMEM((32, 320), f32),
            pltpu.VMEM((320, 320), bf16),
            pltpu.SemaphoreType.DMA((3,)),
        ],
        compiler_params=pltpu.CompilerParams(vmem_limit_bytes=56 << 20),
    )(grad, moment, basis)


def kept_rows(basis, pair, core):
    return jnp.concatenate(
        [basis[za, pair, y, core] for y in Y_ORDER for za in ZA_ORDER], axis=0
    )


def received_rows(received, core):
    return jnp.concatenate(
        [received[za, y, core] for y in Y_ORDER for za in ZA_ORDER], axis=0
    )


def rotate_own_kernel(place, left, basis, received, part):
    core, pair = place[0], place[1]
    part[0] = dot(left[...], kept_rows(basis, pair, core), 0, 0)
    part[1] = dot(left[...], received_rows(received, core), 0, 0)


def rotate_other_kernel(place, left, basis, received, part, sent):
    core, pair = place[0], place[1]
    kept = part[0] + dot(left[...], kept_rows(basis, pair, 1 - core), 0, 0)
    given = part[1] + dot(left[...], received_rows(received, 1 - core), 0, 0)
    for to, total in ((pair, kept.astype(bf16)), (1 - pair, given.astype(bf16))):
        for x in range(X):
            sent[slot(x, to), :80] = total[x * 80 : x * 80 + 80]
            sent[slot(x, to), 80:] = total[320 + x * 80 : 400 + x * 80]


def sum_kernel(parts, second_moment, total, sent):
    value = jnp.sum(parts[...].astype(f32), axis=0)
    total[...] = value
    sent[...] = jnp.concatenate([value, second_moment[...]], axis=0).astype(bf16)


def direction_kernel(place, total, both, second_moment, second, sent):
    upper = place[2] == 0
    partner = both[1 - place[2]].astype(f32)
    summed = total[...] + partner[:160]
    mine, theirs = second_moment[...], partner[160:]
    before = jnp.where(
        upper, jnp.concatenate([mine, theirs], axis=0), jnp.concatenate([theirs, mine], axis=0)
    )
    after = beta_second * before + (1.0 - beta_second) * summed[:80] * summed[:80]
    second[...] = after
    direction = (summed[80:] / (jnp.sqrt(after) + epsilon_root)).astype(bf16)
    for i in range(X * ZB):
        sent[i] = direction


def back_rotate(pair, core, direction, basis, received):
    def columns(which):
        return jnp.concatenate([direction[slot(x, which)] for x in range(X)], axis=0)

    back = dot(columns(pair), kept_rows(basis, pair, core), 1, 1)
    return back + dot(columns(1 - pair), received_rows(received, core), 1, 1)


def back_other_kernel(place, direction, basis, received, sent):
    back = back_rotate(place[1], 1 - place[0], direction, basis, received).astype(bf16)
    for y in range(Y):
        sent[y] = back[:, y * 128 : y * 128 + 128]


def back_own_kernel(place, direction, basis, received, part):
    back = back_rotate(place[1], place[0], direction, basis, received)
    for y in range(Y):
        part[y] = back[:, y * 128 : y * 128 + 128]


def back_add_kernel(part, other, sent):
    sent[...] = (part[...] + other[...].astype(f32)).astype(bf16)


def update_kernel(parts, basis, sent):
    back = jnp.sum(parts[...].astype(f32), axis=0).T.astype(bf16)
    update = dot(back, basis[...], 1, 1).astype(bf16)
    for i in range(ZA):
        block = update[i * 32 : i * 32 + 32]
        sent[i, :32] = block[:, :128]
        sent[i, 32:64] = block[:, 128:256]
        sent[i, 64:] = jnp.concatenate([block[:16, 256:], block[16:, 256:]], axis=1)


def copy_kernel(source, target):
    target[...] = source[...]


def add_kernel(parts, total):
    value = jnp.sum(parts[...].astype(f32), axis=0)
    total[:, :128] = value[:32]
    total[:, 128:256] = value[32:64]
    total[:16, 256:] = value[64:, :64]
    total[16:, 256:] = value[64:, 64:]


def exchange(blocks, axis, order):
    return lax.all_to_all(blocks, axis, 0, 0, axis_index_groups=[list(order)])


def spread(values, axis, order):
    return exchange(jnp.broadcast_to(values[None], (len(order),) + values.shape), axis, order)


def per_device(grad, moment, second_moment, left_basis, right_basis):
    pair = lax.axis_index("zb")
    place = jnp.stack([lax.axis_index("core"), pair, lax.axis_index("zh")])
    momentum, left = left_stage(grad.T, moment.T, left_basis)
    left = exchange(left, "za", ZA_ORDER).reshape(128, 640)
    basis = right_basis.reshape(ZA, ZB, Y, C, 32, 256)
    leaving = lax.dynamic_index_in_dim(basis, 1 - pair, 1, keepdims=False)
    received = lax.ppermute(leaving, "zb", SWAP)
    left = spread(left, "y", Y_ORDER).reshape(512, 640)
    (left,) = local(copy_kernel, (((512, 640), bf16),), (left,))
    left, received = lax.optimization_barrier((left, received))
    left_other = lax.ppermute(left, "core", SWAP)
    (part,) = local(
        rotate_own_kernel, (((ZB, 640, 256), f32),), (place, left, basis, received), 1
    )
    (part,) = local(
        rotate_other_kernel,
        (((X * ZB, 160, 256), bf16),),
        (place, left_other, basis, received, part),
        1,
    )
    part = exchange(part, ("x", "zb"), XZ_ORDER)
    part, sent = local(
        sum_kernel, (((160, 256), f32), ((200, 256), bf16)), (part, second_moment)
    )
    both = lax.all_gather(sent, "zh")
    second, direction = local(
        direction_kernel,
        (((80, 256), f32), ((X * ZB, 80, 256), bf16)),
        (place, part, both, second_moment),
        1,
    )
    direction = exchange(direction, ("x", "zb"), XZ_ORDER)
    blocks = (((Y, 320, 128), bf16),)
    operands = (place, direction, basis, received)
    (sent,) = local(back_other_kernel, blocks, operands, 1)
    other = lax.ppermute(sent, "core", SWAP)
    second = lax.dynamic_slice_in_dim(second, 40 * place[2], 40)
    other, second = lax.optimization_barrier((other, second))
    (part,) = local(back_own_kernel, (((Y, 320, 128), f32),), operands, 1)
    (back,) = local(back_add_kernel, blocks, (part, other))
    back = exchange(back, "y", Y_ORDER)
    (update,) = local(update_kernel, (((ZA, 80, 128), bf16),), (back, left_basis))
    update = exchange(update, "za", ZA_ORDER)
    (update,) = local(add_kernel, (((32, 320), f32),), (update,))
    return (momentum.T, second, update.T)


def solution(mesh):
    names = ("x", "zh", "za", "zb", "y", "core")
    fine = Mesh(mesh.devices.reshape(X, ZH, ZA, ZB, Y, C), names)
    columns = P(None, names)
    block = P(("x", "zh"), ("za", "zb", "y", "core"))
    return jax.shard_map(
        per_device,
        mesh=fine,
        in_specs=(columns, columns, block, P(), block),
        out_specs=(columns, block, columns),
        check_vma=False,
    )
```

```python
import jax
import jax.numpy as jnp
from jax import lax
from jax.experimental import pallas as pl
from jax.experimental.pallas import tpu as pltpu
from jax.sharding import Mesh, PartitionSpec as P

beta_first = 0.95
beta_second = 0.95
epsilon_root = 1e-08

f32 = jnp.float32
bf16 = jnp.bfloat16
X, ZH, ZA, ZB, Y, C = 4, 2, 4, 2, 4, 2
SWAP = [(0, 1), (1, 0)]
ZA_ORDER = (2, 1, 3, 0)
Y_ORDER = (3, 2, 1, 0)
XZ_ORDER = (7, 6, 5, 4, 3, 2, 1, 0)
VMEM = pl.BlockSpec(memory_space=pltpu.VMEM)
HBM = pl.BlockSpec(memory_space=pltpu.HBM)
SMEM = pl.BlockSpec(memory_space=pltpu.SMEM)


def slot(x, pair):
    return X * ZB - 1 - x * ZB - pair


def dot(left, right, over_left, over_right):
    return lax.dot_general(
        left, right, (((over_left,), (over_right,)), ((), ())), preferred_element_type=f32
    )


def local(body, outs, ins, scalars=0):
    shapes = tuple(jax.ShapeDtypeStruct(shape, dtype) for shape, dtype in outs)
    return pl.pallas_call(
        body,
        out_shape=shapes,
        in_specs=[SMEM] * scalars + [VMEM] * (len(ins) - scalars),
        out_specs=(VMEM,) * len(outs),
        compiler_params=pltpu.CompilerParams(vmem_limit_bytes=24 << 20),
    )(*ins)


def left_kernel(grad_hbm, moment_hbm, basis_hbm, momentum, sent, grad, moment, basis, sems):
    pairs = ((grad_hbm, grad), (basis_hbm, basis), (moment_hbm, moment))
    copies = [
        pltpu.make_async_copy(source, target, sems.at[i])
        for i, (source, target) in enumerate(pairs)
    ]
    for copy in copies:
        copy.start()
    for copy in copies:
        copy.wait()
    new = beta_first * moment[...] + (1.0 - beta_first) * grad[...].astype(f32)
    momentum[...] = new
    rotated_grad = dot(grad[...], basis[...], 1, 0).astype(bf16)
    rotated_moment = dot(new.astype(bf16), basis[...], 1, 0).astype(bf16)
    for i in range(ZA):
        sent[i, :, :320] = rotated_grad
        sent[i, :, 320:] = rotated_moment


def left_stage(grad, moment, basis):
    return pl.pallas_call(
        left_kernel,
        out_shape=(
            jax.ShapeDtypeStruct((32, 320), f32),
            jax.ShapeDtypeStruct((ZA, 32, 640), bf16),
        ),
        in_specs=[HBM] * 3,
        out_specs=(VMEM, VMEM),
        scratch_shapes=[
            pltpu.VMEM((32, 320), bf16),
            pltpu.VMEM((32, 320), f32),
            pltpu.VMEM((320, 320), bf16),
            pltpu.SemaphoreType.DMA((3,)),
        ],
        compiler_params=pltpu.CompilerParams(vmem_limit_bytes=56 << 20),
    )(grad, moment, basis)


def kept_rows(basis, pair, core):
    return jnp.concatenate(
        [basis[za, pair, y, core] for y in Y_ORDER for za in ZA_ORDER], axis=0
    )


def received_rows(received, core):
    return jnp.concatenate(
        [received[za, y, core] for y in Y_ORDER for za in ZA_ORDER], axis=0
    )


def rotate_own_kernel(place, left, basis, received, part):
    core, pair = place[0], place[1]
    part[0] = dot(left[...], kept_rows(basis, pair, core), 0, 0)
    part[1] = dot(left[...], received_rows(received, core), 0, 0)


def rotate_other_kernel(place, left, basis, received, part, sent):
    core, pair = place[0], place[1]
    kept = part[0] + dot(left[...], kept_rows(basis, pair, 1 - core), 0, 0)
    given = part[1] + dot(left[...], received_rows(received, 1 - core), 0, 0)
    for to, total in ((pair, kept.astype(bf16)), (1 - pair, given.astype(bf16))):
        for x in range(X):
            sent[slot(x, to), :80] = total[x * 80 : x * 80 + 80]
            sent[slot(x, to), 80:] = total[320 + x * 80 : 400 + x * 80]


def sum_kernel(parts, second_moment, total, sent):
    value = jnp.sum(parts[...].astype(f32), axis=0)
    total[...] = value
    sent[...] = jnp.concatenate([value, second_moment[...]], axis=0).astype(bf16)


def direction_kernel(place, total, both, second_moment, second, sent):
    upper = place[2] == 0
    partner = both[1 - place[2]].astype(f32)
    summed = total[...] + partner[:160]
    mine, theirs = second_moment[...], partner[160:]
    before = jnp.where(
        upper, jnp.concatenate([mine, theirs], axis=0), jnp.concatenate([theirs, mine], axis=0)
    )
    after = beta_second * before + (1.0 - beta_second) * summed[:80] * summed[:80]
    second[...] = after
    direction = (summed[80:] / (jnp.sqrt(after) + epsilon_root)).astype(bf16)
    for i in range(X * ZB):
        sent[i] = direction


def back_rotate(pair, core, direction, basis, received):
    def columns(which):
        return jnp.concatenate([direction[slot(x, which)] for x in range(X)], axis=0)

    back = dot(columns(pair), kept_rows(basis, pair, core), 1, 1)
    return back + dot(columns(1 - pair), received_rows(received, core), 1, 1)


def back_other_kernel(place, direction, basis, received, sent):
    back = back_rotate(place[1], 1 - place[0], direction, basis, received).astype(bf16)
    for y in range(Y):
        sent[y] = back[:, y * 128 : y * 128 + 128]


def back_own_kernel(place, direction, basis, received, part):
    back = back_rotate(place[1], place[0], direction, basis, received)
    for y in range(Y):
        part[y] = back[:, y * 128 : y * 128 + 128]


def back_add_kernel(part, other, sent):
    sent[...] = (part[...] + other[...].astype(f32)).astype(bf16)


def update_kernel(parts, basis, sent):
    back = jnp.sum(parts[...].astype(f32), axis=0).T.astype(bf16)
    update = dot(back, basis[...], 1, 1).astype(bf16)
    for i in range(ZA):
        block = update[i * 32 : i * 32 + 32]
        sent[i, :32] = block[:, :128]
        sent[i, 32:64] = block[:, 128:256]
        sent[i, 64:] = jnp.concatenate([block[:16, 256:], block[16:, 256:]], axis=1)


def copy_kernel(source, target):
    target[...] = source[...]


def add_kernel(parts, total):
    value = jnp.sum(parts[...].astype(f32), axis=0)
    total[:, :128] = value[:32]
    total[:, 128:256] = value[32:64]
    total[:16, 256:] = value[64:, :64]
    total[16:, 256:] = value[64:, 64:]


def exchange(blocks, axis, order):
    return lax.all_to_all(blocks, axis, 0, 0, axis_index_groups=[list(order)])


def spread(values, axis, order):
    return exchange(jnp.broadcast_to(values[None], (len(order),) + values.shape), axis, order)


def per_device(grad, moment, second_moment, left_basis, right_basis):
    pair = lax.axis_index("zb")
    place = jnp.stack([lax.axis_index("core"), pair, lax.axis_index("zh")])
    momentum, left = left_stage(grad.T, moment.T, left_basis)
    left = exchange(left, "za", ZA_ORDER).reshape(128, 640)
    basis = right_basis.reshape(ZA, ZB, Y, C, 32, 256)
    leaving = lax.dynamic_index_in_dim(basis, 1 - pair, 1, keepdims=False)
    received = lax.ppermute(leaving, "zb", SWAP)
    left = spread(left, "y", Y_ORDER).reshape(512, 640)
    (left,) = local(copy_kernel, (((512, 640), bf16),), (left,))
    left, received = lax.optimization_barrier((left, received))
    left_other = lax.ppermute(left, "core", SWAP)
    (part,) = local(
        rotate_own_kernel, (((ZB, 640, 256), f32),), (place, left, basis, received), 1
    )
    (part,) = local(
        rotate_other_kernel,
        (((X * ZB, 160, 256), bf16),),
        (place, left_other, basis, received, part),
        1,
    )
    part = exchange(part, ("x", "zb"), XZ_ORDER)
    part, sent = local(
        sum_kernel, (((160, 256), f32), ((200, 256), bf16)), (part, second_moment)
    )
    both = lax.all_gather(sent, "zh")
    second, direction = local(
        direction_kernel,
        (((80, 256), f32), ((X * ZB, 80, 256), bf16)),
        (place, part, both, second_moment),
        1,
    )
    direction = exchange(direction, ("x", "zb"), XZ_ORDER)
    blocks = (((Y, 320, 128), bf16),)
    operands = (place, direction, basis, received)
    (sent,) = local(back_other_kernel, blocks, operands, 1)
    other = lax.ppermute(sent, "core", SWAP)
    second = lax.dynamic_slice_in_dim(second, 40 * place[2], 40)
    other, second = lax.optimization_barrier((other, second))
    (part,) = local(back_own_kernel, (((Y, 320, 128), f32),), operands, 1)
    (back,) = local(back_add_kernel, blocks, (part, other))
    back = exchange(back, "y", Y_ORDER)
    (update,) = local(update_kernel, (((ZA, 80, 128), bf16),), (back, left_basis))
    update = exchange(update, "za", ZA_ORDER)
    (update,) = local(add_kernel, (((32, 320), f32),), (update,))
    return (momentum.T, second, update.T)


def solution(mesh):
    names = ("x", "zh", "za", "zb", "y", "core")
    fine = Mesh(mesh.devices.reshape(X, ZH, ZA, ZB, Y, C), names)
    columns = P(None, names)
    block = P(("x", "zh"), ("za", "zb", "y", "core"))
    return jax.shard_map(
        per_device,
        mesh=fine,
        in_specs=(columns, columns, block, P(), block),
        out_specs=(columns, block, columns),
        check_vma=False,
    )
```

```python
import jax
import jax.numpy as jnp
from jax import lax
from jax.experimental import pallas as pl
from jax.experimental.pallas import tpu as pltpu
from jax.sharding import Mesh, PartitionSpec as P

beta_first = 0.95
beta_second = 0.95
epsilon_root = 1e-08

f32 = jnp.float32
bf16 = jnp.bfloat16
X, ZH, ZA, ZB, Y, C = 4, 2, 4, 2, 4, 2
SWAP = [(0, 1), (1, 0)]
ZA_ORDER = (2, 1, 3, 0)
Y_ORDER = (2, 1, 3, 0)
X_ORDER = (2, 1, 3, 0)
XZ_ORDER = (4, 5, 2, 3, 6, 7, 0, 1)
VMEM = pl.BlockSpec(memory_space=pltpu.VMEM)
HBM = pl.BlockSpec(memory_space=pltpu.HBM)
SMEM = pl.BlockSpec(memory_space=pltpu.SMEM)


def slot(x, pair):
    return X_ORDER.index(x) * ZB + pair


def dot(left, right, over_left, over_right):
    return lax.dot_general(
        left, right, (((over_left,), (over_right,)), ((), ())), preferred_element_type=f32
    )


def local(body, outs, ins, scalars=0):
    shapes = tuple(jax.ShapeDtypeStruct(shape, dtype) for shape, dtype in outs)
    return pl.pallas_call(
        body,
        out_shape=shapes,
        in_specs=[SMEM] * scalars + [VMEM] * (len(ins) - scalars),
        out_specs=(VMEM,) * len(outs),
        compiler_params=pltpu.CompilerParams(vmem_limit_bytes=24 << 20),
    )(*ins)


def left_kernel(grad_hbm, moment_hbm, basis_hbm, momentum, sent, grad, moment, basis, sems):
    pairs = ((grad_hbm, grad), (basis_hbm, basis), (moment_hbm, moment))
    copies = [
        pltpu.make_async_copy(source, target, sems.at[i])
        for i, (source, target) in enumerate(pairs)
    ]
    for copy in copies:
        copy.start()
    for copy in copies:
        copy.wait()
    new = beta_first * moment[...] + (1.0 - beta_first) * grad[...].astype(f32)
    momentum[...] = new
    rotated_grad = dot(grad[...], basis[...], 1, 0).astype(bf16)
    rotated_moment = dot(new.astype(bf16), basis[...], 1, 0).astype(bf16)
    for i in range(ZA):
        sent[i, :, :320] = rotated_grad
        sent[i, :, 320:] = rotated_moment


def left_stage(grad, moment, basis):
    return pl.pallas_call(
        left_kernel,
        out_shape=(
            jax.ShapeDtypeStruct((32, 320), f32),
            jax.ShapeDtypeStruct((ZA, 32, 640), bf16),
        ),
        in_specs=[HBM] * 3,
        out_specs=(VMEM, VMEM),
        scratch_shapes=[
            pltpu.VMEM((32, 320), bf16),
            pltpu.VMEM((32, 320), f32),
            pltpu.VMEM((320, 320), bf16),
            pltpu.SemaphoreType.DMA((3,)),
        ],
        compiler_params=pltpu.CompilerParams(vmem_limit_bytes=56 << 20),
    )(grad, moment, basis)


def kept_rows(basis, pair, core):
    return jnp.concatenate(
        [basis[za, pair, y, core] for y in Y_ORDER for za in ZA_ORDER], axis=0
    )


def received_rows(received, core):
    return jnp.concatenate(
        [received[za, y, core] for y in Y_ORDER for za in ZA_ORDER], axis=0
    )


def rotate_own_kernel(place, left, basis, received, part):
    core, pair = place[0], place[1]
    part[0] = dot(left[...], kept_rows(basis, pair, core), 0, 0)
    part[1] = dot(left[...], received_rows(received, core), 0, 0)


def rotate_other_kernel(place, left, basis, received, part, sent):
    core, pair = place[0], place[1]
    kept = part[0] + dot(left[...], kept_rows(basis, pair, 1 - core), 0, 0)
    given = part[1] + dot(left[...], received_rows(received, 1 - core), 0, 0)
    for to, total in ((pair, kept.astype(bf16)), (1 - pair, given.astype(bf16))):
        for x in range(X):
            sent[slot(x, to), :80] = total[x * 80 : x * 80 + 80]
            sent[slot(x, to), 80:] = total[320 + x * 80 : 400 + x * 80]


def sum_kernel(parts, second_moment, total, sent):
    value = jnp.sum(parts[...].astype(f32), axis=0)
    total[...] = value
    sent[...] = jnp.concatenate([value, second_moment[...]], axis=0).astype(bf16)


def direction_kernel(place, total, both, second_moment, second, sent):
    upper = place[2] == 0
    partner = both[1 - place[2]].astype(f32)
    summed = total[...] + partner[:160]
    mine, theirs = second_moment[...], partner[160:]
    before = jnp.where(
        upper, jnp.concatenate([mine, theirs], axis=0), jnp.concatenate([theirs, mine], axis=0)
    )
    after = beta_second * before + (1.0 - beta_second) * summed[:80] * summed[:80]
    second[...] = after
    direction = (summed[80:] / (jnp.sqrt(after) + epsilon_root)).astype(bf16)
    for i in range(X * ZB):
        sent[i] = direction


def back_rotate(pair, core, direction, basis, received):
    def columns(which):
        return jnp.concatenate([direction[slot(x, which)] for x in range(X)], axis=0)

    back = dot(columns(pair), kept_rows(basis, pair, core), 1, 1)
    return back + dot(columns(1 - pair), received_rows(received, core), 1, 1)


def back_other_kernel(place, direction, basis, received, sent):
    back = back_rotate(place[1], 1 - place[0], direction, basis, received).astype(bf16)
    for y in range(Y):
        sent[y] = back[:, y * 128 : y * 128 + 128]


def back_own_kernel(place, direction, basis, received, part):
    back = back_rotate(place[1], place[0], direction, basis, received)
    for y in range(Y):
        part[y] = back[:, y * 128 : y * 128 + 128]


def back_add_kernel(part, other, sent):
    sent[...] = (part[...] + other[...].astype(f32)).astype(bf16)


def update_kernel(parts, basis, sent):
    back = jnp.sum(parts[...].astype(f32), axis=0).T.astype(bf16)
    update = dot(back, basis[...], 1, 1).astype(bf16)
    for i in range(ZA):
        block = update[i * 32 : i * 32 + 32]
        sent[i, :32] = block[:, :128]
        sent[i, 32:64] = block[:, 128:256]
        sent[i, 64:] = jnp.concatenate([block[:16, 256:], block[16:, 256:]], axis=1)


def copy_kernel(source, target):
    target[...] = source[...]


def add_kernel(parts, total):
    value = jnp.sum(parts[...].astype(f32), axis=0)
    total[:, :128] = value[:32]
    total[:, 128:256] = value[32:64]
    total[:16, 256:] = value[64:, :64]
    total[16:, 256:] = value[64:, 64:]


def exchange(blocks, axis, order):
    return lax.all_to_all(blocks, axis, 0, 0, axis_index_groups=[list(order)])


def spread(values, axis, order):
    return exchange(jnp.broadcast_to(values[None], (len(order),) + values.shape), axis, order)


def per_device(grad, moment, second_moment, left_basis, right_basis):
    pair = lax.axis_index("zb")
    place = jnp.stack([lax.axis_index("core"), pair, lax.axis_index("zh")])
    momentum, left = left_stage(grad.T, moment.T, left_basis)
    left = exchange(left, "za", ZA_ORDER).reshape(128, 640)
    basis = right_basis.reshape(ZA, ZB, Y, C, 32, 256)
    leaving = lax.dynamic_index_in_dim(basis, 1 - pair, 1, keepdims=False)
    received = lax.ppermute(leaving, "zb", SWAP)
    left = spread(left, "y", Y_ORDER).reshape(512, 640)
    (left,) = local(copy_kernel, (((512, 640), bf16),), (left,))
    left, received = lax.optimization_barrier((left, received))
    left_other = lax.ppermute(left, "core", SWAP)
    (part,) = local(
        rotate_own_kernel, (((ZB, 640, 256), f32),), (place, left, basis, received), 1
    )
    (part,) = local(
        rotate_other_kernel,
        (((X * ZB, 160, 256), bf16),),
        (place, left_other, basis, received, part),
        1,
    )
    part = exchange(part, ("x", "zb"), XZ_ORDER)
    part, sent = local(
        sum_kernel, (((160, 256), f32), ((200, 256), bf16)), (part, second_moment)
    )
    both = lax.all_gather(sent, "zh")
    second, direction = local(
        direction_kernel,
        (((80, 256), f32), ((X * ZB, 80, 256), bf16)),
        (place, part, both, second_moment),
        1,
    )
    direction = exchange(direction, ("x", "zb"), XZ_ORDER)
    blocks = (((Y, 320, 128), bf16),)
    operands = (place, direction, basis, received)
    (sent,) = local(back_other_kernel, blocks, operands, 1)
    other = lax.ppermute(sent, "core", SWAP)
    second = lax.dynamic_slice_in_dim(second, 40 * place[2], 40)
    other, second = lax.optimization_barrier((other, second))
    (part,) = local(back_own_kernel, (((Y, 320, 128), f32),), operands, 1)
    (back,) = local(back_add_kernel, blocks, (part, other))
    back = exchange(back, "y", Y_ORDER)
    (update,) = local(update_kernel, (((ZA, 80, 128), bf16),), (back, left_basis))
    update = exchange(update, "za", ZA_ORDER)
    (update,) = local(add_kernel, (((32, 320), f32),), (update,))
    return (momentum.T, second, update.T)


def solution(mesh):
    names = ("x", "zh", "za", "zb", "y", "core")
    fine = Mesh(mesh.devices.reshape(X, ZH, ZA, ZB, Y, C), names)
    columns = P(None, names)
    block = P(("x", "zh"), ("za", "zb", "y", "core"))
    return jax.shard_map(
        per_device,
        mesh=fine,
        in_specs=(columns, columns, block, P(), block),
        out_specs=(columns, block, columns),
        check_vma=False,
    )
```
